256 devices in a mesh: row: 16 (over z_hi, y, core), col: 16 (over z_lo, x).
Axes of the slice: x: 4, y: 4, z: 8 (z_hi: 2, z_lo: 4; z = z_hi * 4 + z_lo), core: 2. Of those that a mesh axis runs over, the one named last changes fastest.
Arguments:
- features: bfloat16 [32768, 256], P(('col', 'row')), may hold values from -6 to 6
- weight: bfloat16 [256, 256], replicated, may hold values from -0.375 to 0.375
- cotangent: bfloat16 [32768, 256], P(('row', 'col')), may hold values from -6 to 6
- tile_row: int32 [16, 16, 192], P('row', 'col'), may hold values from 0 to 15
- tile_col: int32 [16, 16, 192], P('row', 'col'), may hold values from 0 to 15
- tile_vals: bfloat16 [16, 16, 192, 128, 128], P('row', 'col'), may hold values from -0.0625 to 0.0625
- tile_count: int32 [16, 16], P('row', 'col'), may hold values from 1 to 192, as said below
Outputs:
- output: bfloat16 [32768, 256], P(('row', 'col'))
- weight_grad: float32 [256, 256], replicated
- feature_grad: bfloat16 [32768, 256], P(('col', 'row'))
The draws below stay inside these ranges and needn't reach their ends.
Inputs may be any that keep to these rules, and one draw needn't show every extreme that they name: Only the first tile_count[p, q] slots of block (p, q) hold tiles; the other slots are ignored. Some block has all 192 slots live.
All inputs are finite; a program needn't handle non-finite values.
Results may differ from the reference program's by a relative error of at most 0.03.
Values may be sent and summed in bfloat16 or wider, within the bound.
A program may use at most 128 MiB of HBM per device.

```python
import jax
import jax.numpy as jnp
from jax import lax

F = 256
TILE = 128
ND = 128
TCAP = 192
ROWBLK = 2048
COLBLK = 2048
NODES = 32768
N_ROW = 16
N_COL = 16


def draw_tile_count(key, part):
    key = jax.random.fold_in(key, 7)
    count_key, heavy_key = jax.random.split(key)
    counts = jax.random.randint(count_key, (N_ROW * N_COL,), max(1, TCAP // 8), TCAP // 2 + 1, dtype=jnp.int32)
    heavy_slot = jax.random.randint(heavy_key, (), 0, N_ROW * N_COL, dtype=jnp.int32)
    counts = jnp.where(jnp.arange(N_ROW * N_COL, dtype=jnp.int32) == heavy_slot, TCAP, counts).astype(jnp.int32)
    return counts.reshape(N_ROW, N_COL)


def plant(entries, stream_key, smallest, top_value):
    longest = entries.shape.index(max(entries.shape))
    spots = []
    for shift in (0, 1):
        where = [jax.random.randint(jax.random.fold_in(stream_key, axis), (), 0, length) for axis, length in enumerate(entries.shape)]
        where[longest] = (where[longest] + shift) % entries.shape[longest]
        spots.append(tuple(where))
    return entries.at[spots[0]].set(smallest).at[spots[1]].set(top_value)


def level_of(stream_key, extent, shards, smallest, top_value):
    factor_of, own = 1.0, jax.random.fold_in(stream_key, 6)
    for axis_at, shards_of in shards:
        draws = jnp.exp(jax.random.uniform(jax.random.fold_in(own, axis_at), (shards_of,), jnp.float32, smallest / len(shards), top_value / len(shards)))
        factor_of = factor_of * jnp.repeat(draws, extent[axis_at] // shards_of).reshape([-1 if axis == axis_at else 1 for axis in range(len(extent))])
    return factor_of


def normal_values(rng, extent, spread, reach, cuts=(), kind=jnp.bfloat16):
    level = level_of(rng, extent, cuts, -0.22, 0.18) if cuts else 1.0
    values = jax.random.normal(rng, extent, jnp.float32) * spread * level
    return jnp.minimum(jnp.maximum(values, -reach), reach).astype(kind)


def setup_inputs(seed: int = 0) -> dict:
    arg_keys = jax.random.split(jax.random.key(seed), 8)
    features = normal_values(arg_keys[0], (NODES, F), 1.0, 6.0, ((0, 256),))
    weight = normal_values(arg_keys[1], (F, F), F ** -0.5, 0.375)
    cotangent = normal_values(arg_keys[2], (NODES, F), 1.0, 6.0, ((0, 256),))
    tile_row = plant(jax.random.randint(arg_keys[3], (N_ROW, N_COL, TCAP), 0, ROWBLK // TILE), jax.random.fold_in(arg_keys[3], 1), 0, (ROWBLK // TILE) - 1).astype(jnp.int32)
    tile_col = plant(jax.random.randint(arg_keys[4], (N_ROW, N_COL, TCAP), 0, COLBLK // TILE), jax.random.fold_in(arg_keys[4], 1), 0, (COLBLK // TILE) - 1).astype(jnp.int32)
    tile_vals = normal_values(arg_keys[5], (N_ROW, N_COL, TCAP, TILE, TILE), (max(1, TCAP * TILE * TILE // (3 * ND))) ** -0.5, 0.0625, ((0, 16), (1, 16)))
    tile_count = draw_tile_count(jax.random.fold_in(arg_keys[7], 71), 0)
    return dict(features=features, weight=weight, cotangent=cotangent, tile_row=tile_row, tile_col=tile_col, tile_vals=tile_vals, tile_count=tile_count)


def gelu_parts(pre_act):
    factor = 0.7978845608028654
    inner_arg = factor * (pre_act + 0.044715 * pre_act * pre_act * pre_act)
    tangent_h = jnp.tanh(inner_arg)
    activation = 0.5 * pre_act * (1.0 + tangent_h)
    gradient_slope = 0.5 * (1.0 + tangent_h) + 0.5 * pre_act * (1.0 - tangent_h * tangent_h) * factor * (1.0 + 0.134145 * pre_act * pre_act)
    return activation, gradient_slope


def sweep_tiles(tile_row, tile_col, tile_vals, tile_count, source, backward):
    feat_width = source.shape[1]

    def block_step(index, running):
        block_row = (index // N_COL).astype(jnp.int32)
        block_col = (index % N_COL).astype(jnp.int32)

        def tile_step(slot, inner_run):
            row_at = (block_row * ROWBLK + tile_row[block_row, block_col, slot] * TILE).astype(jnp.int32)
            col_at = (block_col * COLBLK + tile_col[block_row, block_col, slot] * TILE).astype(jnp.int32)
            tile_block = tile_vals[block_row, block_col, slot]
            if backward:
                piece = lax.dynamic_slice_in_dim(source, row_at, TILE, 0)
                product = jnp.dot(tile_block.T, piece, preferred_element_type=jnp.float32)
                target = col_at
            else:
                piece = lax.dynamic_slice_in_dim(source, col_at, TILE, 0)
                product = jnp.dot(tile_block, piece, preferred_element_type=jnp.float32)
                target = row_at
            current = lax.dynamic_slice_in_dim(inner_run, target, TILE, 0)
            return lax.dynamic_update_slice_in_dim(inner_run, current + product, target, 0)

        return lax.fori_loop(jnp.int32(0), tile_count[block_row, block_col].astype(jnp.int32), tile_step, running)

    start = jnp.zeros((NODES, feat_width), jnp.float32)
    return lax.fori_loop(jnp.int32(0), jnp.int32(N_ROW * N_COL), block_step, start)


def reference(features, weight, cotangent, tile_row, tile_col, tile_vals, tile_count):
    aggregated = sweep_tiles(tile_row, tile_col, tile_vals, tile_count, features, False).astype(jnp.bfloat16)
    pre_act = jnp.dot(aggregated, weight, preferred_element_type=jnp.float32)
    activation, gradient_slope = gelu_parts(pre_act)
    output = activation.astype(jnp.bfloat16)
    grad_pre = (cotangent.astype(jnp.float32) * gradient_slope).astype(jnp.bfloat16)
    weight_grad = jnp.dot(aggregated.T, grad_pre, preferred_element_type=jnp.float32) * (NODES ** -0.5)
    grad_agg = jnp.dot(grad_pre, weight.T, preferred_element_type=jnp.float32).astype(jnp.bfloat16)
    feature_grad = sweep_tiles(tile_row, tile_col, tile_vals, tile_count, grad_agg, True).astype(jnp.bfloat16)
    return output, weight_grad, feature_grad
```

```python
import functools

import jax
import jax.numpy as jnp
from jax import lax
from jax.experimental import pallas as pl
from jax.experimental.pallas import tpu as pltpu
from jax.sharding import PartitionSpec as P

MESH = pl.DeviceIdType.MESH
F32 = jnp.float32
BF16 = jnp.bfloat16
N_Y, N_X, N_ZL = 4, 4, 4
TILE, FEAT, SLOTS = 128, 256, 192
BLOCKS = 16


def gelu_parts(pre_act):
    factor = 0.7978845608028654
    square = pre_act * pre_act
    tangent_h = jnp.tanh(factor * (pre_act + 0.044715 * pre_act * square))
    half = 0.5 * (1.0 + tangent_h)
    activation = pre_act * half
    slope = half + 0.5 * pre_act * (1.0 - tangent_h * tangent_h) * factor * (1.0 + 0.134145 * square)
    return activation, slope


def copies():
    names = {}

    def number(*name):
        return names.setdefault(name, len(names))

    return number


N_COPIES = 96


def kernel(
    feat_ref, weight_ref, cot_ref, row_ref, col_ref, vals_ref, count_ref,
    out_ref, wgrad_ref, fgrad_ref,
    tiles, dense_sum, adj, adj_t, keys, index_v, prev_s, last_s,
    feats, part, recv_x, send_z, recv_z, row_agg,
    part_b, recv_c, send_y, recv_y, send_h, recv_h,
    wg, wg_recv_c, wg_v, wg_recv_y, wg_u, wg_recv_x, wg_t, wg_t2, wg_u2, wg_v2,
    load_sem, index_sem, send_sem, recv_sem,
):
    r, q = lax.axis_index("row"), lax.axis_index("col")
    c, y, zh = r % 2, (r // 2) % N_Y, r // (2 * N_Y)
    x, zl = q % N_X, q // N_X

    def at(y=y, c=c, zh=zh, x=x, zl=zl):
        return (zh * (2 * N_Y) + y * 2 + c, zl * N_X + x)

    def row_of(y=y, c=c, zh=zh):
        return at(y, c, zh)[0]

    def col_of(x=x, zl=zl):
        return at(x=x, zl=zl)[1]

    def plus(v, k):
        return (v + k) % 4

    core_peer, high_peer = at(c=1 - c), at(zh=1 - zh)
    y_peer = {k: at(y=plus(y, k)) for k in (1, 2, 3)}
    x_peer = {k: at(x=plus(x, k)) for k in (1, 2, 3)}
    z_peer = {k: at(zl=plus(zl, k)) for k in (1, 2, 3)}

    number = copies()

    def send(name, src, dst, peer):
        i = number(*name)
        pltpu.make_async_remote_copy(
            src_ref=src, dst_ref=dst, send_sem=send_sem.at[i], recv_sem=recv_sem.at[i],
            device_id=peer, device_id_type=MESH,
        ).start()
        pending.append((i, src, peer))

    def arrived(name, dst):
        i = number(*name)
        pltpu.make_async_remote_copy(
            src_ref=dst, dst_ref=dst, send_sem=send_sem.at[i], recv_sem=recv_sem.at[i],
            device_id=core_peer, device_id_type=MESH,
        ).wait_recv()

    pending = []

    load = pltpu.make_async_copy(vals_ref, tiles, load_sem.at[0])
    load.start()

    barrier = pltpu.get_barrier_semaphore()
    peers = [core_peer, high_peer] + [p[k] for p in (y_peer, x_peer, z_peer) for k in (1, 2, 3)]
    for peer in peers:
        pl.semaphore_signal(barrier, inc=1, device_id=peer, device_id_type=MESH)
    pl.semaphore_wait(barrier, len(peers))

    own = feats.at[r]
    send(("f_h",), feat_ref, own, high_peer)
    for k in (2, 1, 3):
        send(("f_y", k), feat_ref, own, y_peer[k])
    send(("f_c", 0, 0), feat_ref, own, core_peer)
    feats[r] = feat_ref[...]

    keys[...] = jnp.full(keys.shape, -1, jnp.int32)
    keys[0:1, 0:SLOTS] = row_ref[...] * BLOCKS + col_ref[...]
    key_row = jnp.broadcast_to(keys[0:1, :], (256, 256))
    key_col = key_row.T
    at_t = lax.broadcasted_iota(jnp.int32, (256, 256), 0)
    at_s = lax.broadcasted_iota(jnp.int32, (256, 256), 1)
    before = jnp.max(jnp.where((key_col == key_row) & (at_t < at_s), at_t, -1), axis=0, keepdims=True)
    newest = jnp.max(jnp.where((key_col == at_s) & (at_t < count_ref[0, 0]), at_t, -1), axis=0, keepdims=True)
    index_v[0] = jnp.where(before < 0, SLOTS, before)
    index_v[1] = jnp.where(newest < 0, SLOTS, newest)
    first = pltpu.make_async_copy(index_v.at[0], prev_s, index_sem.at[0])
    second = pltpu.make_async_copy(index_v.at[1], last_s, index_sem.at[1])
    first.start()
    second.start()
    first.wait()
    second.wait()
    load.wait()

    other = row_of(zh=1 - zh)
    arrived(("f_h",), feats.at[other])
    for k in (2, 1, 3):
        send(("f_hy", k), feats.at[other], feats.at[other], y_peer[k])
    send(("f_c", 1, 0), feats.at[other], feats.at[other], core_peer)

    dense_sum[SLOTS] = jnp.zeros((TILE, TILE), F32)

    def add_slot(s, carry):
        dense_sum[s] = dense_sum[jnp.clip(prev_s[0, s], 0, SLOTS)] + tiles[s].astype(F32)
        return carry

    lax.fori_loop(0, SLOTS, add_slot, 0)

    for k in (1, 3, 2):
        near = row_of(y=plus(y, -k))
        arrived(("f_y", k), feats.at[near])
        send(("f_c", 0, k), feats.at[near], feats.at[near], core_peer)

    def fill_row(i, carry):
        for j in range(BLOCKS):
            adj[i, :, j * TILE:(j + 1) * TILE] = dense_sum[jnp.clip(last_s[0, i * BLOCKS + j], 0, SLOTS)].astype(BF16)
        return carry

    lax.fori_loop(0, BLOCKS, fill_row, 0)

    for k in (1, 3, 2):
        far = row_of(y=plus(y, -k), zh=1 - zh)
        arrived(("f_hy", k), feats.at[far])
        send(("f_c", 1, k), feats.at[far], feats.at[far], core_peer)
    for h in (0, 1):
        for k in (0, 1, 3, 2):
            src = row_of(y=plus(y, -k), c=1 - c, zh=zh if h == 0 else 1 - zh)
            arrived(("f_c", h, k), feats.at[src])

    source = feats[...].reshape(BLOCKS * TILE, FEAT)
    for kz in (2, 1, 3, 0):
        to = plus(zl, kz)
        rows = adj[pl.ds(to * N_X, N_X)].reshape(N_X * TILE, BLOCKS * TILE)
        part[to] = jnp.dot(rows, source, preferred_element_type=F32).astype(BF16).reshape(N_X, TILE, FEAT)
        for kx in (2, 1, 3):
            send(("p_x", kx, kz), part.at[to, plus(x, kx)], recv_x.at[kx - 1, to], x_peer[kx])

    def turn_row(i, carry):
        for j in range(BLOCKS):
            adj_t[i, :, j * TILE:(j + 1) * TILE] = adj[j, :, pl.ds(pl.multiple_of(i * TILE, TILE), TILE)].T
        return carry

    lax.fori_loop(0, BLOCKS // 2, turn_row, 0)

    for kz in (2, 1, 3, 0):
        to = plus(zl, kz)
        for kx in (1, 3, 2):
            arrived(("p_x", kx, kz), recv_x.at[kx - 1, to])
        total = part[to, x].astype(F32) + recv_x[0, to].astype(F32) + recv_x[1, to].astype(F32) + recv_x[2, to].astype(F32)
        if kz:
            send_z[kz - 1] = total.astype(BF16)
            send(("p_z", kz), send_z.at[kz - 1], recv_z.at[kz - 1], z_peer[kz])

    lax.fori_loop(BLOCKS // 2, BLOCKS, turn_row, 0)

    for kz in (1, 3, 2):
        arrived(("p_z", kz), recv_z.at[kz - 1])
        total = total + recv_z[kz - 1].astype(F32)
    aggregated = total.astype(BF16)

    weight = weight_ref[...]
    pre_act = jnp.dot(aggregated, weight, preferred_element_type=F32)
    activation, slope = gelu_parts(pre_act)
    grad_pre = (cot_ref[...].astype(F32) * slope).astype(BF16)
    grad_agg = lax.dot_general(grad_pre, weight, (((1,), (1,)), ((), ())), preferred_element_type=F32)
    row_agg[q] = grad_agg.astype(BF16)

    own = row_agg.at[q]
    for kz in (2, 1, 3):
        send(("g_z", kz), own, own, z_peer[kz])
    for kx in (2, 1, 3):
        send(("g_x", 0, kx), own, own, x_peer[kx])
    out_ref[...] = activation.astype(BF16)
    wg[...] = lax.dot_general(
        aggregated, grad_pre, (((0,), (0,)), ((), ())), preferred_element_type=F32
    ).reshape(2, TILE, FEAT)
    send(("w_c",), wg.at[1 - c], wg_recv_c, core_peer)

    for kz in (1, 3, 2):
        near = col_of(zl=plus(zl, -kz))
        arrived(("g_z", kz), row_agg.at[near])
        for kx in (2, 1, 3):
            send(("g_x", kz, kx), row_agg.at[near], row_agg.at[near], x_peer[kx])

    arrived(("w_c",), wg_recv_c)
    wg_v[...] = (wg[c] + wg_recv_c[...]).reshape(N_Y, TILE // N_Y, FEAT)
    for k in (2, 1, 3):
        send(("w_y", k), wg_v.at[plus(y, k)], wg_recv_y.at[k - 1], y_peer[k])
    for kx in (1, 3, 2):
        arrived(("g_x", 0, kx), row_agg.at[col_of(x=plus(x, -kx))])
    for k in (1, 3, 2):
        arrived(("w_y", k), wg_recv_y.at[k - 1])
    wg_u[...] = (wg_v[y] + wg_recv_y[0] + wg_recv_y[1] + wg_recv_y[2]).reshape(N_X, 8, FEAT)
    for k in (2, 1, 3):
        send(("w_x", k), wg_u.at[plus(x, k)], wg_recv_x.at[k - 1], x_peer[k])

    for kz in (1, 3, 2):
        for kx in (1, 3, 2):
            arrived(("g_x", kz, kx), row_agg.at[col_of(x=plus(x, -kx), zl=plus(zl, -kz))])

    source_b = row_agg[...].reshape(BLOCKS * TILE, FEAT)

    def backward(to_c, to_h, dst):
        for j in range(N_Y):
            rows = adj_t[to_h * (2 * N_Y) + j * 2 + to_c]
            dst[j] = jnp.dot(rows, source_b, preferred_element_type=F32).astype(BF16)

    for i, (to_c, to_h) in enumerate(((1 - c, 1 - zh), (1 - c, zh), (c, 1 - zh), (c, zh))):
        backward(to_c, to_h, part_b.at[i])
        if i < 2:
            send(("b_c", i), part_b.at[i], recv_c.at[i], core_peer)
        if i == 1:
            for k in (1, 3, 2):
                arrived(("w_x", k), wg_recv_x.at[k - 1])
            wg_t[zl] = wg_u[x] + wg_recv_x[0] + wg_recv_x[1] + wg_recv_x[2]
            for k in (2, 1, 3):
                send(("w_z", k), wg_t.at[zl], wg_t.at[zl], z_peer[k])
        if i >= 2:
            h = i - 2
            arrived(("b_c", h), recv_c.at[h])
            send_y[h] = (part_b[i].astype(F32) + recv_c[h].astype(F32)).astype(BF16)
            for k in (2, 1, 3):
                send(("b_y", h, k), send_y.at[h, plus(y, k)], recv_y.at[h, k - 1], y_peer[k])

    for k in (1, 3, 2):
        arrived(("w_z", k), wg_t.at[plus(zl, -k)])
    wg_t2[zh] = (wg_t[0] + wg_t[1]) + (wg_t[2] + wg_t[3])
    send(("w_h",), wg_t2.at[zh], wg_t2.at[zh], high_peer)

    for h in (0, 1):
        for k in (1, 3, 2):
            arrived(("b_y", h, k), recv_y.at[h, k - 1])
        total = send_y[h, y].astype(F32) + recv_y[h, 0].astype(F32) + recv_y[h, 1].astype(F32) + recv_y[h, 2].astype(F32)
        if h == 0:
            send_h[...] = total.astype(BF16)
            send(("b_h",), send_h, recv_h, high_peer)

    arrived(("w_h",), wg_t2.at[1 - zh])
    wg_u2[x] = wg_t2[0] + wg_t2[1]
    for k in (2, 1, 3):
        send(("w_xb", k), wg_u2.at[x], wg_u2.at[x], x_peer[k])
    for k in (1, 3, 2):
        arrived(("w_xb", k), wg_u2.at[plus(x, -k)])
    wg_v2[y] = wg_u2[...].reshape(TILE // N_Y, FEAT)
    for k in (2, 1, 3):
        send(("w_yb", k), wg_v2.at[y], wg_v2.at[y], y_peer[k])

    arrived(("b_h",), recv_h)
    fgrad_ref[...] = (total + recv_h[...].astype(F32)).astype(BF16)

    for k in (1, 3, 2):
        arrived(("w_yb", k), wg_v2.at[plus(y, -k)])
    wgrad_ref[c] = wg_v2[...].reshape(TILE, FEAT)
    send(("w_cb",), wgrad_ref.at[c], wgrad_ref.at[c], core_peer)
    arrived(("w_cb",), wgrad_ref.at[1 - c])

    for i, src, peer in pending:
        pltpu.make_async_remote_copy(
            src_ref=src, dst_ref=src, send_sem=send_sem.at[i], recv_sem=recv_sem.at[i],
            device_id=peer, device_id_type=MESH,
        ).wait_send()


def body(features, weight, cotangent, tile_row, tile_col, tile_vals, tile_count):
    node_total = 32768
    vmem, smem = pl.BlockSpec(memory_space=pltpu.VMEM), pl.BlockSpec(memory_space=pltpu.SMEM)
    output, weight_sum, feature_grad = pl.pallas_call(
        kernel,
        out_shape=(
            jax.ShapeDtypeStruct((TILE, FEAT), BF16),
            jax.ShapeDtypeStruct((2, TILE, FEAT), F32),
            jax.ShapeDtypeStruct((TILE, FEAT), BF16),
        ),
        in_specs=[vmem, vmem, vmem, vmem, vmem, pl.BlockSpec(memory_space=pl.ANY), smem],
        out_specs=(vmem, vmem, vmem),
        scratch_shapes=[
            pltpu.VMEM((SLOTS, TILE, TILE), BF16),
            pltpu.VMEM((SLOTS + 1, TILE, TILE), F32),
            pltpu.VMEM((BLOCKS, TILE, BLOCKS * TILE), BF16),
            pltpu.VMEM((BLOCKS, TILE, BLOCKS * TILE), BF16),
            pltpu.VMEM((8, 256), jnp.int32),
            pltpu.VMEM((2, 1, 256), jnp.int32),
            pltpu.SMEM((1, 256), jnp.int32),
            pltpu.SMEM((1, 256), jnp.int32),
            pltpu.VMEM((BLOCKS, TILE, FEAT), BF16),
            pltpu.VMEM((N_ZL, N_X, TILE, FEAT), BF16),
            pltpu.VMEM((3, N_ZL, TILE, FEAT), BF16),
            pltpu.VMEM((3, TILE, FEAT), BF16),
            pltpu.VMEM((3, TILE, FEAT), BF16),
            pltpu.VMEM((BLOCKS, TILE, FEAT), BF16),
            pltpu.VMEM((4, N_Y, TILE, FEAT), BF16),
            pltpu.VMEM((2, N_Y, TILE, FEAT), BF16),
            pltpu.VMEM((2, N_Y, TILE, FEAT), BF16),
            pltpu.VMEM((2, 3, TILE, FEAT), BF16),
            pltpu.VMEM((TILE, FEAT), BF16),
            pltpu.VMEM((TILE, FEAT), BF16),
            pltpu.VMEM((2, TILE, FEAT), F32),
            pltpu.VMEM((TILE, FEAT), F32),
            pltpu.VMEM((N_Y, TILE // N_Y, FEAT), F32),
            pltpu.VMEM((3, TILE // N_Y, FEAT), F32),
            pltpu.VMEM((N_X, 8, FEAT), F32),
            pltpu.VMEM((3, 8, FEAT), F32),
            pltpu.VMEM((N_ZL, 8, FEAT), F32),
            pltpu.VMEM((2, 8, FEAT), F32),
            pltpu.VMEM((N_X, 8, FEAT), F32),
            pltpu.VMEM((N_Y, TILE // N_Y, FEAT), F32),
            pltpu.SemaphoreType.DMA((1,)),
            pltpu.SemaphoreType.DMA((2,)),
            pltpu.SemaphoreType.DMA((N_COPIES,)),
            pltpu.SemaphoreType.DMA((N_COPIES,)),
        ],
        compiler_params=pltpu.CompilerParams(
            collective_id=0, has_side_effects=True, vmem_limit_bytes=60 * 1024 * 1024
        ),
        name="layer",
    )(features, weight, cotangent, tile_row[0], tile_col[0], tile_vals[0, 0], tile_count)
    weight_grad = weight_sum.reshape(FEAT, FEAT) * node_total ** (-0.5)
    return output, weight_grad, feature_grad


def solution(mesh):
    in_specs = (
        P(("col", "row"), None),
        P(),
        P(("row", "col"), None),
        P("row", "col", None),
        P("row", "col", None),
        P("row", "col", None, None, None),
        P("row", "col"),
    )
    out_specs = (P(("row", "col"), None), P(), P(("col", "row"), None))
    return jax.shard_map(body, mesh=mesh, in_specs=in_specs, out_specs=out_specs, check_vma=False)
```

```python
import functools

import jax
import jax.numpy as jnp
from jax import lax
from jax.experimental import pallas as pl
from jax.experimental.pallas import tpu as pltpu
from jax.sharding import PartitionSpec as P

MESH = pl.DeviceIdType.MESH
F32 = jnp.float32
BF16 = jnp.bfloat16
N_Y, N_X, N_ZL = 4, 4, 4
TILE, FEAT, SLOTS = 128, 256, 192
BLOCKS = 16


def gelu_parts(pre_act):
    factor = 0.7978845608028654
    square = pre_act * pre_act
    tangent_h = jnp.tanh(factor * (pre_act + 0.044715 * pre_act * square))
    half = 0.5 * (1.0 + tangent_h)
    activation = pre_act * half
    slope = half + 0.5 * pre_act * (1.0 - tangent_h * tangent_h) * factor * (1.0 + 0.134145 * square)
    return activation, slope


def copies():
    names = {}

    def number(*name):
        return names.setdefault(name, len(names))

    return number


N_COPIES = 96


def kernel(
    scale, feat_ref, weight_hbm, cot_hbm, row_hbm, col_hbm, vals_ref, count_hbm,
    out_ref, wgrad_ref, fgrad_ref,
    weight_ref, cot_ref, row_ref, col_ref, count_ref,
    tiles, dense_sum, adj, adj_t, keys, index_v, prev_s, last_s,
    feats, part, recv_x, send_z, recv_z, row_agg,
    part_b, recv_c, send_y, recv_y, send_h, recv_h,
    wg, wg_recv_c, wg_v, wg_recv_y, wg_u, wg_recv_z, wg_t, wg_t2, wg_u2, wg_v2,
    load_sem, index_sem, send_sem, recv_sem,
):
    r, q = lax.axis_index("row"), lax.axis_index("col")
    c, y, zh = r % 2, (r // 2) % N_Y, r // (2 * N_Y)
    x, zl = q % N_X, q // N_X

    def at(y=y, c=c, zh=zh, x=x, zl=zl):
        return (zh * (2 * N_Y) + y * 2 + c, zl * N_X + x)

    def row_of(y=y, c=c, zh=zh):
        return at(y, c, zh)[0]

    def col_of(x=x, zl=zl):
        return at(x=x, zl=zl)[1]

    def plus(v, k):
        return (v + k) % 4

    core_peer, high_peer = at(c=1 - c), at(zh=1 - zh)
    y_peer = {k: at(y=plus(y, k)) for k in (1, 2, 3)}
    x_peer = {k: at(x=plus(x, k)) for k in (1, 2, 3)}
    z_peer = {k: at(zl=plus(zl, k)) for k in (1, 2, 3)}

    number = copies()

    def send(name, src, dst, peer):
        i = number(*name)
        pltpu.make_async_remote_copy(
            src_ref=src, dst_ref=dst, send_sem=send_sem.at[i], recv_sem=recv_sem.at[i],
            device_id=peer, device_id_type=MESH,
        ).start()
        pending.append((i, src, peer))

    def arrived(name, dst):
        i = number(*name)
        pltpu.make_async_remote_copy(
            src_ref=dst, dst_ref=dst, send_sem=send_sem.at[i], recv_sem=recv_sem.at[i],
            device_id=core_peer, device_id_type=MESH,
        ).wait_recv()

    pending = []

    own = feats.at[r]
    loads = {}
    for i, (src, dst) in enumerate((
        (row_hbm, row_ref), (col_hbm, col_ref), (count_hbm, count_ref), (feat_ref, own),
        (weight_hbm, weight_ref), (cot_hbm, cot_ref), (vals_ref, tiles),
    )):
        loads[i] = pltpu.make_async_copy(src, dst, load_sem.at[i])
        loads[i].start()

    barrier = pltpu.get_barrier_semaphore()
    peers = [core_peer, high_peer] + [p[k] for p in (y_peer, x_peer, z_peer) for k in (1, 2, 3)]
    for peer in peers:
        pl.semaphore_signal(barrier, inc=1, device_id=peer, device_id_type=MESH)
    pl.semaphore_wait(barrier, len(peers))

    send(("f_h",), feat_ref, own, high_peer)
    for k in (2, 1, 3):
        send(("f_y", k), feat_ref, own, y_peer[k])
    send(("f_c", 0, 0), feat_ref, own, core_peer)

    for i in range(3):
        loads[i].wait()
    keys[...] = jnp.full(keys.shape, -1, jnp.int32)
    keys[0:1, 0:SLOTS] = row_ref[...] * BLOCKS + col_ref[...]
    key_row = jnp.broadcast_to(keys[0:1, :], (256, 256))
    key_col = key_row.T
    at_t = lax.broadcasted_iota(jnp.int32, (256, 256), 0)
    at_s = lax.broadcasted_iota(jnp.int32, (256, 256), 1)
    before = jnp.max(jnp.where((key_col == key_row) & (at_t < at_s), at_t, -1), axis=0, keepdims=True)
    newest = jnp.max(jnp.where((key_col == at_s) & (at_t < count_ref[0, 0]), at_t, -1), axis=0, keepdims=True)
    index_v[0] = jnp.where(before < 0, SLOTS, before)
    index_v[1] = jnp.where(newest < 0, SLOTS, newest)
    first = pltpu.make_async_copy(index_v.at[0], prev_s, index_sem.at[0])
    second = pltpu.make_async_copy(index_v.at[1], last_s, index_sem.at[1])
    first.start()
    second.start()
    first.wait()
    second.wait()
    for i in range(3, 7):
        loads[i].wait()

    other = row_of(zh=1 - zh)
    arrived(("f_h",), feats.at[other])
    for k in (2, 1, 3):
        send(("f_hy", k), feats.at[other], feats.at[other], y_peer[k])
    send(("f_c", 1, 0), feats.at[other], feats.at[other], core_peer)

    dense_sum[SLOTS] = jnp.zeros((TILE, TILE), F32)

    def add_slot(s, carry):
        dense_sum[s] = dense_sum[jnp.clip(prev_s[0, s], 0, SLOTS)] + tiles[s].astype(F32)
        return carry

    lax.fori_loop(0, SLOTS, add_slot, 0)

    for k in (1, 3, 2):
        near = row_of(y=plus(y, -k))
        arrived(("f_y", k), feats.at[near])
        send(("f_c", 0, k), feats.at[near], feats.at[near], core_peer)

    def fill_row(i, carry):
        for j in range(BLOCKS):
            adj[i, :, j * TILE:(j + 1) * TILE] = dense_sum[jnp.clip(last_s[0, i * BLOCKS + j], 0, SLOTS)].astype(BF16)
        return carry

    lax.fori_loop(0, BLOCKS, fill_row, 0)

    for k in (1, 3, 2):
        far = row_of(y=plus(y, -k), zh=1 - zh)
        arrived(("f_hy", k), feats.at[far])
        send(("f_c", 1, k), feats.at[far], feats.at[far], core_peer)
    for h in (0, 1):
        for k in (0, 1, 3, 2):
            src = row_of(y=plus(y, -k), c=1 - c, zh=zh if h == 0 else 1 - zh)
            arrived(("f_c", h, k), feats.at[src])

    source = feats[...].reshape(BLOCKS * TILE, FEAT)
    for kz in (2, 1, 3, 0):
        to = plus(zl, kz)
        rows = adj[pl.ds(to * N_X, N_X)].reshape(N_X * TILE, BLOCKS * TILE)
        part[to] = jnp.dot(rows, source, preferred_element_type=F32).astype(BF16).reshape(N_X, TILE, FEAT)
        for kx in (2, 1, 3):
            send(("p_x", kx, kz), part.at[to, plus(x, kx)], recv_x.at[kx - 1, to], x_peer[kx])

    def turn_row(i, carry):
        for j in range(BLOCKS):
            adj_t[i, :, j * TILE:(j + 1) * TILE] = adj[j, :, pl.ds(pl.multiple_of(i * TILE, TILE), TILE)].T
        return carry

    lax.fori_loop(0, BLOCKS // 2, turn_row, 0)

    for kz in (2, 1, 3, 0):
        to = plus(zl, kz)
        for kx in (1, 3, 2):
            arrived(("p_x", kx, kz), recv_x.at[kx - 1, to])
        total = part[to, x].astype(F32) + recv_x[0, to].astype(F32) + recv_x[1, to].astype(F32) + recv_x[2, to].astype(F32)
        if kz:
            send_z[kz - 1] = total.astype(BF16)
            send(("p_z", kz), send_z.at[kz - 1], recv_z.at[kz - 1], z_peer[kz])

    lax.fori_loop(BLOCKS // 2, BLOCKS, turn_row, 0)

    for kz in (1, 3, 2):
        arrived(("p_z", kz), recv_z.at[kz - 1])
        total = total + recv_z[kz - 1].astype(F32)
    aggregated = total.astype(BF16)

    weight = weight_ref[...]
    pre_act = jnp.dot(aggregated, weight, preferred_element_type=F32)
    activation, slope = gelu_parts(pre_act)
    grad_pre = (cot_ref[...].astype(F32) * slope).astype(BF16)
    grad_agg = lax.dot_general(grad_pre, weight, (((1,), (1,)), ((), ())), preferred_element_type=F32)
    row_agg[q] = grad_agg.astype(BF16)

    own = row_agg.at[q]
    for kz in (2, 1, 3):
        send(("g_z", kz), own, own, z_peer[kz])
    for kx in (2, 1, 3):
        send(("g_x", 0, kx), own, own, x_peer[kx])
    out_ref[...] = activation.astype(BF16)
    wg[...] = lax.dot_general(
        aggregated, grad_pre, (((0,), (0,)), ((), ())), preferred_element_type=F32
    ).reshape(2, TILE, FEAT)
    send(("w_c",), wg.at[1 - c], wg_recv_c, core_peer)

    for kz in (1, 3, 2):
        near = col_of(zl=plus(zl, -kz))
        arrived(("g_z", kz), row_agg.at[near])
        for kx in (2, 1, 3):
            send(("g_x", kz, kx), row_agg.at[near], row_agg.at[near], x_peer[kx])
        if kz == 1:
            arrived(("w_c",), wg_recv_c)
            wg_v[...] = (wg[c] + wg_recv_c[...]).reshape(N_Y, TILE // N_Y, FEAT)
            for k in (2, 1, 3):
                send(("w_y", k), wg_v.at[plus(y, k)], wg_recv_y.at[k - 1], y_peer[k])

    for k in (1, 3, 2):
        arrived(("w_y", k), wg_recv_y.at[k - 1])
    wg_u[...] = (wg_v[y] + wg_recv_y[0] + wg_recv_y[1] + wg_recv_y[2]).reshape(N_ZL, 8, FEAT)
    for k in (2, 1, 3):
        send(("w_z", k), wg_u.at[plus(zl, k)], wg_recv_z.at[k - 1], z_peer[k])

    for kz in (0, 1, 3, 2):
        for kx in (1, 3, 2):
            arrived(("g_x", kz, kx), row_agg.at[col_of(x=plus(x, -kx), zl=plus(zl, -kz))])
        if kz == 1:
            for k in (1, 3, 2):
                arrived(("w_z", k), wg_recv_z.at[k - 1])
            wg_t[zh] = wg_u[zl] + wg_recv_z[0] + wg_recv_z[1] + wg_recv_z[2]
            send(("w_h",), wg_t.at[zh], wg_t.at[zh], high_peer)

    source_b = row_agg[...].reshape(BLOCKS * TILE, FEAT)

    def backward(to_c, to_h, dst):
        for j in range(N_Y):
            rows = adj_t[to_h * (2 * N_Y) + j * 2 + to_c]
            dst[j] = jnp.dot(rows, source_b, preferred_element_type=F32).astype(BF16)

    for i, (to_c, to_h) in enumerate(((1 - c, 1 - zh), (c, 1 - zh), (1 - c, zh), (c, zh))):
        backward(to_c, to_h, part_b.at[i])
        h = i // 2
        if i in (0, 2):
            send(("b_c", h), part_b.at[i], recv_c.at[h], core_peer)
        else:
            arrived(("b_c", h), recv_c.at[h])
            send_y[h] = (part_b[i].astype(F32) + recv_c[h].astype(F32)).astype(BF16)
            for k in (2, 1, 3):
                send(("b_y", h, k), send_y.at[h, plus(y, k)], recv_y.at[h, k - 1], y_peer[k])
        if i == 0:
            arrived(("w_h",), wg_t.at[1 - zh])
            wg_t2[x] = wg_t[0] + wg_t[1]
            for k in (2, 1, 3):
                send(("w_x", k), wg_t2.at[x], wg_t2.at[x], x_peer[k])

    for k in (1, 3, 2):
        arrived(("w_x", k), wg_t2.at[plus(x, -k)])
    wg_u2[zl] = ((wg_t2[0] + wg_t2[1]) + (wg_t2[2] + wg_t2[3])) * scale
    for k in (2, 1, 3):
        send(("w_zb", k), wg_u2.at[zl], wg_u2.at[zl], z_peer[k])

    for h in (0, 1):
        for k in (1, 3, 2):
            arrived(("b_y", h, k), recv_y.at[h, k - 1])
        total = send_y[h, y].astype(F32) + recv_y[h, 0].astype(F32) + recv_y[h, 1].astype(F32) + recv_y[h, 2].astype(F32)
        if h == 0:
            send_h[...] = total.astype(BF16)
            send(("b_h",), send_h, recv_h, high_peer)
            for k in (1, 3, 2):
                arrived(("w_zb", k), wg_u2.at[plus(zl, -k)])
            wg_v2[y] = wg_u2[...].reshape(TILE // N_Y, FEAT)
            for k in (2, 1, 3):
                send(("w_yb", k), wg_v2.at[y], wg_v2.at[y], y_peer[k])

    for k in (1, 3, 2):
        arrived(("w_yb", k), wg_v2.at[plus(y, -k)])
    wgrad_ref[c] = wg_v2[...].reshape(TILE, FEAT)
    send(("w_cb",), wgrad_ref.at[c], wgrad_ref.at[c], core_peer)

    arrived(("b_h",), recv_h)
    fgrad_ref[...] = (total + recv_h[...].astype(F32)).astype(BF16)
    arrived(("w_cb",), wgrad_ref.at[1 - c])

    for i, src, peer in pending:
        pltpu.make_async_remote_copy(
            src_ref=src, dst_ref=src, send_sem=send_sem.at[i], recv_sem=recv_sem.at[i],
            device_id=peer, device_id_type=MESH,
        ).wait_send()


def hand_over(out_src, wgrad_src, fgrad_src, out_dst, wgrad_dst, fgrad_dst, sem):
    pairs = ((out_src, out_dst), (wgrad_src, wgrad_dst), (fgrad_src, fgrad_dst))
    moves = [pltpu.make_async_copy(src, dst, sem.at[i]) for i, (src, dst) in enumerate(pairs)]
    for move in moves:
        move.start()
    for move in moves:
        move.wait()


def body(features, weight, cotangent, tile_row, tile_col, tile_vals, tile_count):
    whole = pl.BlockSpec(memory_space=pl.ANY)
    scale = (BLOCKS * BLOCKS * TILE) ** -0.5
    out_shape = (
        jax.ShapeDtypeStruct((TILE, FEAT), BF16),
        jax.ShapeDtypeStruct((2, TILE, FEAT), F32),
        jax.ShapeDtypeStruct((TILE, FEAT), BF16),
    )
    results = pl.pallas_call(
        functools.partial(kernel, scale),
        out_shape=out_shape,
        in_specs=[whole] * 7,
        out_specs=(pl.BlockSpec(memory_space=pltpu.VMEM),) * 3,
        scratch_shapes=[
            pltpu.VMEM((FEAT, FEAT), BF16),
            pltpu.VMEM((TILE, FEAT), BF16),
            pltpu.VMEM((1, SLOTS), jnp.int32),
            pltpu.VMEM((1, SLOTS), jnp.int32),
            pltpu.SMEM((1, 1), jnp.int32),
            pltpu.VMEM((SLOTS, TILE, TILE), BF16),
            pltpu.VMEM((SLOTS + 1, TILE, TILE), F32),
            pltpu.VMEM((BLOCKS, TILE, BLOCKS * TILE), BF16),
            pltpu.VMEM((BLOCKS, TILE, BLOCKS * TILE), BF16),
            pltpu.VMEM((8, 256), jnp.int32),
            pltpu.VMEM((2, 1, 256), jnp.int32),
            pltpu.SMEM((1, 256), jnp.int32),
            pltpu.SMEM((1, 256), jnp.int32),
            pltpu.VMEM((BLOCKS, TILE, FEAT), BF16),
            pltpu.VMEM((N_ZL, N_X, TILE, FEAT), BF16),
            pltpu.VMEM((3, N_ZL, TILE, FEAT), BF16),
            pltpu.VMEM((3, TILE, FEAT), BF16),
            pltpu.VMEM((3, TILE, FEAT), BF16),
            pltpu.VMEM((BLOCKS, TILE, FEAT), BF16),
            pltpu.VMEM((4, N_Y, TILE, FEAT), BF16),
            pltpu.VMEM((2, N_Y, TILE, FEAT), BF16),
            pltpu.VMEM((2, N_Y, TILE, FEAT), BF16),
            pltpu.VMEM((2, 3, TILE, FEAT), BF16),
            pltpu.VMEM((TILE, FEAT), BF16),
            pltpu.VMEM((TILE, FEAT), BF16),
            pltpu.VMEM((2, TILE, FEAT), F32),
            pltpu.VMEM((TILE, FEAT), F32),
            pltpu.VMEM((N_Y, TILE // N_Y, FEAT), F32),
            pltpu.VMEM((3, TILE // N_Y, FEAT), F32),
            pltpu.VMEM((N_ZL, 8, FEAT), F32),
            pltpu.VMEM((3, 8, FEAT), F32),
            pltpu.VMEM((2, 8, FEAT), F32),
            pltpu.VMEM((N_X, 8, FEAT), F32),
            pltpu.VMEM((N_ZL, 8, FEAT), F32),
            pltpu.VMEM((N_Y, TILE // N_Y, FEAT), F32),
            pltpu.SemaphoreType.DMA((10,)),
            pltpu.SemaphoreType.DMA((2,)),
            pltpu.SemaphoreType.DMA((N_COPIES,)),
            pltpu.SemaphoreType.DMA((N_COPIES,)),
        ],
        compiler_params=pltpu.CompilerParams(
            collective_id=0, has_side_effects=True, vmem_limit_bytes=62 * 1024 * 1024
        ),
        name="layer",
    )(features, weight, cotangent, tile_row[0], tile_col[0], tile_vals[0, 0], tile_count)
    output, weight_grad, feature_grad = pl.pallas_call(
        hand_over,
        out_shape=out_shape,
        in_specs=[pl.BlockSpec(memory_space=pltpu.VMEM)] * 3,
        out_specs=(whole,) * 3,
        scratch_shapes=[pltpu.SemaphoreType.DMA((3,))],
        name="hand_over",
    )(*results)
    return output, weight_grad.reshape(FEAT, FEAT), feature_grad


def solution(mesh):
    in_specs = (
        P(("col", "row"), None),
        P(),
        P(("row", "col"), None),
        P("row", "col", None),
        P("row", "col", None),
        P("row", "col", None, None, None),
        P("row", "col"),
    )
    out_specs = (P(("row", "col"), None), P(), P(("col", "row"), None))
    return jax.shard_map(body, mesh=mesh, in_specs=in_specs, out_specs=out_specs, check_vma=False)
```

```python
import functools

import jax
import jax.numpy as jnp
from jax import lax
from jax.experimental import pallas as pl
from jax.experimental.pallas import tpu as pltpu
from jax.sharding import PartitionSpec as P

MESH = pl.DeviceIdType.MESH
F32 = jnp.float32
BF16 = jnp.bfloat16
N_Y, N_X, N_ZL = 4, 4, 4
TILE, FEAT, SLOTS = 128, 256, 192
BLOCKS = 16
SPLIT = 64


def gelu_parts(pre_act):
    factor = 0.7978845608028654
    square = pre_act * pre_act
    tangent_h = jnp.tanh(factor * (pre_act + 0.044715 * pre_act * square))
    half = 0.5 * (1.0 + tangent_h)
    activation = pre_act * half
    slope = half + 0.5 * pre_act * (1.0 - tangent_h * tangent_h) * factor * (1.0 + 0.134145 * square)
    return activation, slope


def copies():
    names = {}

    def number(*name):
        return names.setdefault(name, len(names))

    return number


N_COPIES = 104


def kernel(
    scale, feat_ref, weight_hbm, cot_hbm, row_hbm, col_hbm, vals_ref, count_hbm,
    out_ref, wgrad_ref, fgrad_ref,
    weight_ref, cot_ref, row_ref, col_ref, count_ref,
    tiles, dense_sum, adj, adj_t, keys, index_v, prev_s, last_s,
    feats, part, recv_x, send_z, recv_z, row_agg,
    part_b, recv_c, send_y, recv_y, send_h, recv_h,
    wg, wg_recv_c, wg_v, wg_recv_y, wg_u, wg_recv_z, wg_t, wg_t2, wg_u2, wg_v2, grown,
    load_sem, index_sem, send_sem, recv_sem,
):
    r, q = lax.axis_index("row"), lax.axis_index("col")
    c, y, zh = r % 2, (r // 2) % N_Y, r // (2 * N_Y)
    x, zl = q % N_X, q // N_X

    def at(y=y, c=c, zh=zh, x=x, zl=zl):
        return (zh * (2 * N_Y) + y * 2 + c, zl * N_X + x)

    def row_of(y=y, c=c, zh=zh):
        return at(y, c, zh)[0]

    def col_of(x=x, zl=zl):
        return at(x=x, zl=zl)[1]

    def plus(v, k):
        return (v + k) % 4

    core_peer, high_peer = at(c=1 - c), at(zh=1 - zh)
    y_peer = {k: at(y=plus(y, k)) for k in (1, 2, 3)}
    x_peer = {k: at(x=plus(x, k)) for k in (1, 2, 3)}
    z_peer = {k: at(zl=plus(zl, k)) for k in (1, 2, 3)}

    number = copies()

    def send(name, src, dst, peer):
        i = number(*name)
        pltpu.make_async_remote_copy(
            src_ref=src, dst_ref=dst, send_sem=send_sem.at[i], recv_sem=recv_sem.at[i],
            device_id=peer, device_id_type=MESH,
        ).start()
        pending.append((i, src, peer))

    def arrived(name, dst):
        i = number(*name)
        pltpu.make_async_remote_copy(
            src_ref=dst, dst_ref=dst, send_sem=send_sem.at[i], recv_sem=recv_sem.at[i],
            device_id=core_peer, device_id_type=MESH,
        ).wait_recv()

    pending = []

    own = feats.at[r]
    loads = {}
    for i, (src, dst) in enumerate((
        (row_hbm, row_ref), (col_hbm, col_ref), (count_hbm, count_ref), (feat_ref, own),
        (weight_hbm, weight_ref), (cot_hbm, cot_ref), (vals_ref, tiles),
    )):
        loads[i] = pltpu.make_async_copy(src, dst, load_sem.at[i])
        loads[i].start()

    barrier = pltpu.get_barrier_semaphore()
    peers = [core_peer, high_peer] + [p[k] for p in (y_peer, x_peer, z_peer) for k in (1, 2, 3)]
    for peer in peers:
        pl.semaphore_signal(barrier, inc=1, device_id=peer, device_id_type=MESH)
    pl.semaphore_wait(barrier, len(peers))

    send(("f_h",), feat_ref, own, high_peer)
    for k in (2, 1, 3):
        send(("f_y", k), feat_ref, own, y_peer[k])
    send(("f_c", 0, 0), feat_ref, own, core_peer)

    for i in range(3):
        loads[i].wait()
    keys[...] = jnp.full(keys.shape, -1, jnp.int32)
    keys[0:1, 0:SLOTS] = row_ref[...] * BLOCKS + col_ref[...]
    key_row = jnp.broadcast_to(keys[0:1, :], (256, 256))
    key_col = key_row.T
    at_t = lax.broadcasted_iota(jnp.int32, (256, 256), 0)
    at_s = lax.broadcasted_iota(jnp.int32, (256, 256), 1)
    before = jnp.max(jnp.where((key_col == key_row) & (at_t < at_s), at_t, -1), axis=0, keepdims=True)
    newest = jnp.max(jnp.where((key_col == at_s) & (at_t < count_ref[0, 0]), at_t, -1), axis=0, keepdims=True)
    index_v[0] = jnp.where(before < 0, SLOTS, before)
    index_v[1] = jnp.where(newest < 0, SLOTS, newest)
    first = pltpu.make_async_copy(index_v.at[0], prev_s, index_sem.at[0])
    second = pltpu.make_async_copy(index_v.at[1], last_s, index_sem.at[1])
    first.start()
    second.start()
    first.wait()
    second.wait()
    for i in range(3, 7):
        loads[i].wait()

    other = row_of(zh=1 - zh)
    arrived(("f_h",), feats.at[other])
    for k in (2, 1, 3):
        send(("f_hy", k), feats.at[other], feats.at[other], y_peer[k])
    send(("f_c", 1, 0), feats.at[other], feats.at[other], core_peer)

    dense_sum[SLOTS] = jnp.zeros((TILE, TILE), F32)

    def add_slot(s, carry):
        dense_sum[s] = dense_sum[jnp.clip(prev_s[0, s], 0, SLOTS)] + tiles[s].astype(F32)
        return carry

    lax.fori_loop(0, SLOTS, add_slot, 0)

    for k in (1, 3, 2):
        near = row_of(y=plus(y, -k))
        arrived(("f_y", k), feats.at[near])
        send(("f_c", 0, k), feats.at[near], feats.at[near], core_peer)

    def fill_row(i, carry):
        for j in range(BLOCKS):
            adj[i, :, j * TILE:(j + 1) * TILE] = dense_sum[jnp.clip(last_s[0, i * BLOCKS + j], 0, SLOTS)].astype(BF16)
        return carry

    lax.fori_loop(0, BLOCKS, fill_row, 0)

    for k in (1, 3, 2):
        far = row_of(y=plus(y, -k), zh=1 - zh)
        arrived(("f_hy", k), feats.at[far])
        send(("f_c", 1, k), feats.at[far], feats.at[far], core_peer)
    for h in (0, 1):
        for k in (0, 1, 3, 2):
            src = row_of(y=plus(y, -k), c=1 - c, zh=zh if h == 0 else 1 - zh)
            arrived(("f_c", h, k), feats.at[src])

    for kz in (2, 1, 3, 0):
        to = plus(zl, kz)
        rows = adj[pl.ds(to * N_X, N_X)].reshape(N_X * TILE, BLOCKS * TILE)
        part[to] = jnp.dot(rows, feats[...].reshape(BLOCKS * TILE, FEAT), preferred_element_type=F32).astype(BF16).reshape(N_X, TILE, FEAT)
        for kx in (2, 1, 3):
            send(("p_x", kx, kz), part.at[to, plus(x, kx)], recv_x.at[kx - 1, to], x_peer[kx])

    def turn_row(i, carry):
        for j in range(BLOCKS):
            adj_t[(i % 2) * (BLOCKS // 2) + i // 2, :, j * TILE:(j + 1) * TILE] = adj[j, :, pl.ds(pl.multiple_of(i * TILE, TILE), TILE)].T
        return carry

    lax.fori_loop(0, BLOCKS // 2, turn_row, 0)

    for kz in (2, 1, 3, 0):
        to = plus(zl, kz)
        for kx in (1, 3, 2):
            arrived(("p_x", kx, kz), recv_x.at[kx - 1, to])
        total = part[to, x].astype(F32) + recv_x[0, to].astype(F32) + recv_x[1, to].astype(F32) + recv_x[2, to].astype(F32)
        if kz:
            send_z[kz - 1] = total.astype(BF16)
            send(("p_z", kz), send_z.at[kz - 1], recv_z.at[kz - 1], z_peer[kz])

    lax.fori_loop(BLOCKS // 2, BLOCKS, turn_row, 0)

    for kz in (1, 3, 2):
        arrived(("p_z", kz), recv_z.at[kz - 1])
        total = total + recv_z[kz - 1].astype(F32)
    aggregated = total.astype(BF16)

    weight = weight_ref[...]
    pre_act = jnp.dot(aggregated, weight, preferred_element_type=F32)
    activation, slope = gelu_parts(pre_act)
    grad_pre = (cot_ref[...].astype(F32) * slope).astype(BF16)
    grad_agg = lax.dot_general(grad_pre, weight, (((1,), (1,)), ((), ())), preferred_element_type=F32)
    row_agg[q] = grad_agg.astype(BF16)

    own = row_agg.at[q]
    for kz in (2, 1, 3):
        send(("g_z", kz), own, own, z_peer[kz])
    for kx in (2, 1, 3):
        send(("g_x", 0, kx), own, own, x_peer[kx])
    out_ref[...] = activation.astype(BF16)
    wg[...] = lax.dot_general(
        aggregated, grad_pre, (((0,), (0,)), ((), ())), preferred_element_type=F32
    ).reshape(2, TILE, FEAT)
    send(("w_c",), wg.at[1 - c], wg_recv_c, core_peer)

    arrived(("w_c",), wg_recv_c)
    wg_v[...] = (wg[c] + wg_recv_c[...]).reshape(N_Y, TILE // N_Y, FEAT)
    for k in (2, 1, 3):
        send(("w_y", k), wg_v.at[plus(y, k)], wg_recv_y.at[k - 1], y_peer[k])
    for kz in (1, 3, 2):
        near = col_of(zl=plus(zl, -kz))
        arrived(("g_z", kz), row_agg.at[near])
        for kx in (1, 3):
            send(("g_x", kz, kx), row_agg.at[near], row_agg.at[near], x_peer[kx])
        piece = row_agg.at[near, pl.ds(0, SPLIT)]
        send(("g_x", kz, 2), piece, piece, x_peer[2])
        if kz == 1:
            arrived(("g_x", 0, 2), row_agg.at[col_of(x=plus(x, 2))])
            piece = row_agg.at[col_of(x=plus(x, 2)), pl.ds(SPLIT, TILE - SPLIT)]
            for k in (2, 1, 3):
                send(("g_w", k), piece, piece, z_peer[k])

    for k in (1, 3, 2):
        arrived(("w_y", k), wg_recv_y.at[k - 1])
    wg_u[...] = (wg_v[y] + wg_recv_y[0] + wg_recv_y[1] + wg_recv_y[2]).reshape(N_ZL, 8, FEAT)
    for k in (2, 1, 3):
        send(("w_z", k), wg_u.at[plus(zl, k)], wg_recv_z.at[k - 1], z_peer[k])

    def quarter(kz, group):
        at_z = plus(zl, -kz)
        rows = adj_t[pl.ds(group * N_Y, N_Y), :, pl.ds(pl.multiple_of(at_z * N_X * TILE, TILE), N_X * TILE)]
        known = row_agg[pl.ds(at_z * N_X, N_X)].reshape(N_X * TILE, FEAT)
        return jnp.dot(rows.reshape(N_Y * TILE, N_X * TILE), known, preferred_element_type=F32)

    def arrived_quarter(kz):
        for kx in (1, 3):
            arrived(("g_x", kz, kx), row_agg.at[col_of(x=plus(x, -kx), zl=plus(zl, -kz))])
        if kz:
            there = col_of(x=plus(x, 2), zl=plus(zl, -kz))
            arrived(("g_x", kz, 2), row_agg.at[there, pl.ds(0, SPLIT)])
            arrived(("g_w", kz), row_agg.at[there, pl.ds(SPLIT, TILE - SPLIT)])

    def start(group, carry):
        grown[group] = quarter(0, group) + quarter(1, group) + quarter(3, group)
        return carry

    def grow(kz, group, carry):
        grown[group] += quarter(kz, group)
        return carry

    arrived_quarter(0)
    for kz in (1, 3):
        arrived_quarter(kz)
        if kz == 1:
            for k in (1, 3, 2):
                arrived(("w_z", k), wg_recv_z.at[k - 1])
            wg_t[zh] = wg_u[zl] + wg_recv_z[0] + wg_recv_z[1] + wg_recv_z[2]
            send(("w_h",), wg_t.at[zh], wg_t.at[zh], high_peer)
    lax.fori_loop(0, 4, start, 0)
    arrived_quarter(2)
    for i, (to_c, to_h) in enumerate(((1 - c, 1 - zh), (c, 1 - zh), (1 - c, zh), (c, zh))):
        group = to_c * 2 + to_h
        part_b[i] = (grown[group] + quarter(2, group)).astype(BF16).reshape(N_Y, TILE, FEAT)
        h = i // 2
        if i in (0, 2):
            send(("b_c", h), part_b.at[i], recv_c.at[h], core_peer)
        else:
            arrived(("b_c", h), recv_c.at[h])
            send_y[h] = (part_b[i].astype(F32) + recv_c[h].astype(F32)).astype(BF16)
            for k in (2, 1, 3):
                send(("b_y", h, k), send_y.at[h, plus(y, k)], recv_y.at[h, k - 1], y_peer[k])
        if i == 2:
            for k in (1, 3, 2):
                arrived(("w_x", k), wg_t2.at[plus(x, -k)])
            wg_u2[zl] = ((wg_t2[0] + wg_t2[1]) + (wg_t2[2] + wg_t2[3])) * scale
            for k in (2, 1, 3):
                send(("w_zb", k), wg_u2.at[zl], wg_u2.at[zl], z_peer[k])
        if i == 0:
            arrived(("w_h",), wg_t.at[1 - zh])
            wg_t2[x] = wg_t[0] + wg_t[1]
            for k in (2, 1, 3):
                send(("w_x", k), wg_t2.at[x], wg_t2.at[x], x_peer[k])


    def sum_y(h):
        for k in (1, 3, 2):
            arrived(("b_y", h, k), recv_y.at[h, k - 1])
        return send_y[h, y].astype(F32) + recv_y[h, 0].astype(F32) + recv_y[h, 1].astype(F32) + recv_y[h, 2].astype(F32)

    send_h[...] = sum_y(0).astype(BF16)
    send(("b_h",), send_h, recv_h, high_peer)
    for k in (1, 3, 2):
        arrived(("w_zb", k), wg_u2.at[plus(zl, -k)])
    wg_v2[y] = wg_u2[...].reshape(TILE // N_Y, FEAT)
    for k in (2, 1, 3):
        send(("w_yb", k), wg_v2.at[y], wg_v2.at[y], y_peer[k])
    total = sum_y(1)

    for k in (1, 3, 2):
        arrived(("w_yb", k), wg_v2.at[plus(y, -k)])
    wgrad_ref[c] = wg_v2[...].reshape(TILE, FEAT)
    send(("w_cb",), wgrad_ref.at[c], wgrad_ref.at[c], core_peer)

    arrived(("b_h",), recv_h)
    fgrad_ref[...] = (total + recv_h[...].astype(F32)).astype(BF16)
    arrived(("w_cb",), wgrad_ref.at[1 - c])

    for i, src, peer in pending:
        pltpu.make_async_remote_copy(
            src_ref=src, dst_ref=src, send_sem=send_sem.at[i], recv_sem=recv_sem.at[i],
            device_id=peer, device_id_type=MESH,
        ).wait_send()


def hand_over(out_src, wgrad_src, fgrad_src, out_dst, wgrad_dst, fgrad_dst, sem):
    pairs = ((out_src, out_dst), (wgrad_src, wgrad_dst), (fgrad_src, fgrad_dst))
    moves = [pltpu.make_async_copy(src, dst, sem.at[i]) for i, (src, dst) in enumerate(pairs)]
    for move in moves:
        move.start()
    for move in moves:
        move.wait()


def body(features, weight, cotangent, tile_row, tile_col, tile_vals, tile_count):
    whole = pl.BlockSpec(memory_space=pl.ANY)
    scale = (BLOCKS * BLOCKS * TILE) ** -0.5
    out_shape = (
        jax.ShapeDtypeStruct((TILE, FEAT), BF16),
        jax.ShapeDtypeStruct((2, TILE, FEAT), F32),
        jax.ShapeDtypeStruct((TILE, FEAT), BF16),
    )
    results = pl.pallas_call(
        functools.partial(kernel, scale),
        out_shape=out_shape,
        in_specs=[whole] * 7,
        out_specs=(pl.BlockSpec(memory_space=pltpu.VMEM),) * 3,
        scratch_shapes=[
            pltpu.VMEM((FEAT, FEAT), BF16),
            pltpu.VMEM((TILE, FEAT), BF16),
            pltpu.VMEM((1, SLOTS), jnp.int32),
            pltpu.VMEM((1, SLOTS), jnp.int32),
            pltpu.SMEM((1, 1), jnp.int32),
            pltpu.VMEM((SLOTS, TILE, TILE), BF16),
            pltpu.VMEM((SLOTS + 1, TILE, TILE), F32),
            pltpu.VMEM((BLOCKS, TILE, BLOCKS * TILE), BF16),
            pltpu.VMEM((BLOCKS, TILE, BLOCKS * TILE), BF16),
            pltpu.VMEM((8, 256), jnp.int32),
            pltpu.VMEM((2, 1, 256), jnp.int32),
            pltpu.SMEM((1, 256), jnp.int32),
            pltpu.SMEM((1, 256), jnp.int32),
            pltpu.VMEM((BLOCKS, TILE, FEAT), BF16),
            pltpu.VMEM((N_ZL, N_X, TILE, FEAT), BF16),
            pltpu.VMEM((3, N_ZL, TILE, FEAT), BF16),
            pltpu.VMEM((3, TILE, FEAT), BF16),
            pltpu.VMEM((3, TILE, FEAT), BF16),
            pltpu.VMEM((BLOCKS, TILE, FEAT), BF16),
            pltpu.VMEM((4, N_Y, TILE, FEAT), BF16),
            pltpu.VMEM((2, N_Y, TILE, FEAT), BF16),
            pltpu.VMEM((2, N_Y, TILE, FEAT), BF16),
            pltpu.VMEM((2, 3, TILE, FEAT), BF16),
            pltpu.VMEM((TILE, FEAT), BF16),
            pltpu.VMEM((TILE, FEAT), BF16),
            pltpu.VMEM((2, TILE, FEAT), F32),
            pltpu.VMEM((TILE, FEAT), F32),
            pltpu.VMEM((N_Y, TILE // N_Y, FEAT), F32),
            pltpu.VMEM((3, TILE // N_Y, FEAT), F32),
            pltpu.VMEM((N_ZL, 8, FEAT), F32),
            pltpu.VMEM((3, 8, FEAT), F32),
            pltpu.VMEM((2, 8, FEAT), F32),
            pltpu.VMEM((N_X, 8, FEAT), F32),
            pltpu.VMEM((N_ZL, 8, FEAT), F32),
            pltpu.VMEM((N_Y, TILE // N_Y, FEAT), F32),
            pltpu.VMEM((4, N_Y * TILE, FEAT), F32),
            pltpu.SemaphoreType.DMA((10,)),
            pltpu.SemaphoreType.DMA((2,)),
            pltpu.SemaphoreType.DMA((N_COPIES,)),
            pltpu.SemaphoreType.DMA((N_COPIES,)),
        ],
        compiler_params=pltpu.CompilerParams(
            collective_id=0, has_side_effects=True, vmem_limit_bytes=62 * 1024 * 1024
        ),
        name="layer",
    )(features, weight, cotangent, tile_row[0], tile_col[0], tile_vals[0, 0], tile_count)
    output, weight_grad, feature_grad = pl.pallas_call(
        hand_over,
        out_shape=out_shape,
        in_specs=[pl.BlockSpec(memory_space=pltpu.VMEM)] * 3,
        out_specs=(whole,) * 3,
        scratch_shapes=[pltpu.SemaphoreType.DMA((3,))],
        name="hand_over",
    )(*results)
    return output, weight_grad.reshape(FEAT, FEAT), feature_grad


def solution(mesh):
    in_specs = (
        P(("col", "row"), None),
        P(),
        P(("row", "col"), None),
        P("row", "col", None),
        P("row", "col", None),
        P("row", "col", None, None, None),
        P("row", "col"),
    )
    out_specs = (P(("row", "col"), None), P(), P(("col", "row"), None))
    return jax.shard_map(body, mesh=mesh, in_specs=in_specs, out_specs=out_specs, check_vma=False)
```
